32 devices in a mesh: dp: 4 (over y, x), seq: 8 (over z, core).
Axes of the slice: x: 2, y: 2, z: 4, core: 2. Of those that a mesh axis runs over, the one named last changes fastest.
Arguments:
- binned_signals: bfloat16 [4, 4096, 768], P('dp', 'seq'), may hold values from -6 to 6
- kernel_coefficients: bfloat16 [5, 768, 768], P(None, 'dp'), may hold values from -0.09375 to 0.09375
- asking_projector: bfloat16 [768, 256], replicated, may hold values from -0.21875 to 0.21875
- lookup_projector: bfloat16 [768, 256], replicated, may hold values from -0.21875 to 0.21875
- content_projector: bfloat16 [768, 384], replicated, may hold values from -0.21875 to 0.21875
- readout_projector: bfloat16 [384, 768], replicated, may hold values from -0.3125 to 0.3125
- logit_multipliers: float32 [4], replicated, may hold values from 8 to 24
- loss_sensitivity: bfloat16 [4, 1024, 768], P('dp', 'seq'), may hold values from -0.09375 to 0.09375
Outputs:
- pooled: bfloat16 [4, 1024, 768], P('dp', 'seq')
- update: float32 [4, 1024, 768], P('dp', 'seq')
- query_grad: float32 [768, 256], replicated
- out_grad: float32 [384, 768], replicated
The draws below stay inside these ranges and needn't reach their ends.
All inputs are finite; a program needn't handle non-finite values.
Results may differ from the reference program's by a relative error of at most 0.0095.
The reference program's roundings to bfloat16 on the way count: a program that leaves them out, or rounds other values in their place, can miss the bound.
Values may be sent and summed in bfloat16 or wider, within the bound.
A program may use at most 128 MiB of HBM per device.

```python
import math
import jax
import jax.numpy as jnp
from jax import lax

C = 768
TAPS = 5
POOL = 4
LEARNED_ATTENDS = 4
ATTN_PROBE_SPAN = 64
VALUE_SIZE = 96
TOKENS = 1024
BATCH = 4


def block_levels(key, extent, shards, low, top_value):
    loudness = 1.0
    for position, blocks in shards:
        draws = jax.random.uniform(jax.random.fold_in(jax.random.fold_in(key, 6), position), (blocks,), jnp.float32, low / len(shards), top_value / len(shards))
        loudness = loudness * jnp.repeat(jnp.exp(draws), extent[position] // blocks).reshape((-1,) + (1,) * (len(extent) - 1 - position))
    return loudness


def bell_draw(rng, extent, deviation, bound, split=(), kind=jnp.bfloat16):
    drawn = jax.random.normal(rng, extent, jnp.float32) * deviation
    if len(split) > 0:
        drawn = block_levels(rng, extent, split, -0.22, 0.18) * drawn
    return jnp.clip(drawn, min=-bound, max=bound).astype(kind)


def setup_inputs(seed: int = 0) -> dict:
    splits = jax.random.split(jax.random.key(seed), 9)
    binned_signals = bell_draw(splits[0], (BATCH, POOL * TOKENS, C), 1.0, 6.0, ((0, 4), (1, 8)))
    kernel_coefficients = bell_draw(splits[1], (TAPS, C, C), (TAPS * C) ** -0.5, 0.09375, ((1, 4),))
    asking_projector = bell_draw(splits[2], (C, LEARNED_ATTENDS * ATTN_PROBE_SPAN), C ** -0.5, 0.21875)
    lookup_projector = bell_draw(splits[3], (C, LEARNED_ATTENDS * ATTN_PROBE_SPAN), C ** -0.5, 0.21875)
    content_projector = bell_draw(splits[4], (C, LEARNED_ATTENDS * VALUE_SIZE), C ** -0.5, 0.21875)
    readout_projector = bell_draw(splits[5], (LEARNED_ATTENDS * VALUE_SIZE, C), (LEARNED_ATTENDS * VALUE_SIZE) ** -0.5, 0.3125)
    logit_multipliers = jnp.clip(jnp.exp(jax.random.uniform(splits[6], (LEARNED_ATTENDS,), jnp.float32, math.log(8.0), math.log(24.0))), 8.0, 24.0)
    loss_sensitivity = bell_draw(splits[7], (BATCH, TOKENS, C), (BATCH * TOKENS) ** -0.5, 0.09375, ((0, 4), (1, 8)))
    return dict(binned_signals=binned_signals, kernel_coefficients=kernel_coefficients, asking_projector=asking_projector, lookup_projector=lookup_projector, content_projector=content_projector, readout_projector=readout_projector, logit_multipliers=logit_multipliers, loss_sensitivity=loss_sensitivity)


norm_eps = 1e-05
head_eps = 1e-06

def layer_norm(values):
    centre = lax.optimization_barrier(jnp.mean(values, axis=-1, keepdims=True))
    shifted = values - centre
    variance = lax.optimization_barrier(jnp.mean(shifted * shifted, axis=-1, keepdims=True))
    return shifted * lax.rsqrt(variance + norm_eps)

def activate(values):
    return values * jax.nn.sigmoid(1.702 * values)

def head_norm(values, group_width):
    grouped = values.reshape(values.shape[0], -1, group_width)
    factor = lax.rsqrt(lax.optimization_barrier(jnp.mean(grouped * grouped, axis=-1, keepdims=True)) + head_eps)
    return ((grouped * factor).reshape(values.shape), jnp.broadcast_to(factor, grouped.shape).reshape(values.shape))

def contract_first(former, latter):
    return lax.dot_general(former, latter, (((0,), (0,)), ((), ())), preferred_element_type=jnp.float32)

def contract_last(former, latter):
    return lax.dot_general(former, latter, (((1,), (1,)), ((), ())), preferred_element_type=jnp.float32)

def lone_genome_strand(incoming_tensor, kernel_coefficients, asking_projector, lookup_projector, content_projector, readout_projector, logit_multipliers, directional_perturbations):
    length_fine = incoming_tensor.shape[0]
    channels = incoming_tensor.shape[1]
    margin = TAPS // 2
    activated = activate(layer_norm(incoming_tensor.astype(jnp.float32))).astype(jnp.bfloat16)
    padded = jnp.pad(activated, ((margin, margin), (0, 0)))
    conv_sum = jnp.zeros((length_fine, channels), jnp.float32)
    for tap_index in range(TAPS):
        conv_sum = conv_sum + jnp.dot(padded[tap_index:tap_index + length_fine], kernel_coefficients[tap_index], preferred_element_type=jnp.float32)
    summed = incoming_tensor.astype(jnp.float32) + conv_sum
    pooled = lax.optimization_barrier(jnp.max(summed.reshape(length_fine // POOL, POOL, channels), axis=1)).astype(jnp.bfloat16)
    normed = layer_norm(pooled.astype(jnp.float32)).astype(jnp.bfloat16)
    queries = jnp.dot(normed, asking_projector, preferred_element_type=jnp.float32)
    query_hat, query_factor = head_norm(queries, ATTN_PROBE_SPAN)
    query_unit = query_hat.astype(jnp.bfloat16)
    key_unit = head_norm(jnp.dot(normed, lookup_projector, preferred_element_type=jnp.float32), ATTN_PROBE_SPAN)[0].astype(jnp.bfloat16)
    values_all = jnp.dot(normed, content_projector, preferred_element_type=jnp.float32).astype(jnp.bfloat16)
    heads_grad = contract_last(directional_perturbations, readout_projector).astype(jnp.bfloat16)
    outputs = []
    diffs = []
    for attender_slot in range(LEARNED_ATTENDS):
        key_lo = attender_slot * ATTN_PROBE_SPAN
        value_lo = attender_slot * VALUE_SIZE
        query_part = query_unit[:, key_lo:key_lo + ATTN_PROBE_SPAN]
        key_part = key_unit[:, key_lo:key_lo + ATTN_PROBE_SPAN]
        value_part = values_all[:, value_lo:value_lo + VALUE_SIZE]
        attender_logit_gain = logit_multipliers[attender_slot] / ATTN_PROBE_SPAN
        scores = contract_last(query_part, key_part) * attender_logit_gain
        expo = jnp.exp(scores)
        probs = expo / lax.optimization_barrier(jnp.sum(expo, axis=1, keepdims=True))
        head_out = jnp.dot(probs.astype(jnp.bfloat16), value_part, preferred_element_type=jnp.float32)
        outputs.append(head_out)
        grad_part = heads_grad[:, value_lo:value_lo + VALUE_SIZE]
        prob_grad = contract_last(grad_part, value_part)
        delta = lax.optimization_barrier(jnp.sum(grad_part.astype(jnp.float32) * head_out, axis=1, keepdims=True))
        score_grad = (probs * (prob_grad - delta)).astype(jnp.bfloat16)
        unit_grad = jnp.dot(score_grad, key_part, preferred_element_type=jnp.float32) * attender_logit_gain
        hat_part = query_hat[:, key_lo:key_lo + ATTN_PROBE_SPAN]
        factor_part = query_factor[:, key_lo:key_lo + ATTN_PROBE_SPAN]
        diffs.append(factor_part * (unit_grad - hat_part * lax.optimization_barrier(jnp.mean(hat_part * unit_grad, axis=1, keepdims=True))))
    heads_low = jnp.concatenate(outputs, axis=1).astype(jnp.bfloat16)
    update = jnp.dot(heads_low, readout_projector, preferred_element_type=jnp.float32)
    query_diff = jnp.concatenate(diffs, axis=1).astype(jnp.bfloat16)
    return (pooled, update, contract_first(normed, query_diff), contract_first(heads_low, directional_perturbations))

def reference(binned_signals, kernel_coefficients, asking_projector, lookup_projector, content_projector, readout_projector, logit_multipliers, loss_sensitivity):

    def per_item(coupled_entries):
        return lone_genome_strand(coupled_entries[0], kernel_coefficients, asking_projector, lookup_projector, content_projector, readout_projector, logit_multipliers, coupled_entries[1])
    pooled, update, query_parts, out_parts = lax.map(per_item, (binned_signals, loss_sensitivity))
    return (pooled, update, lax.optimization_barrier(jnp.sum(query_parts, axis=0)), lax.optimization_barrier(jnp.sum(out_parts, axis=0)))
```

```python
import functools
import math

import jax
import jax.numpy as jnp
from jax import lax
from jax.experimental import pallas as pl
from jax.experimental.pallas import tpu as pltpu
from jax.sharding import PartitionSpec as P

POOL = 4
LANES = 128
norm_eps = 1e-05
head_eps = 1e-06
F32 = jnp.float32
BF16 = jnp.bfloat16
MESH = pl.DeviceIdType.MESH


def layer_norm(values):
    centre = jnp.mean(values, axis=-1, keepdims=True)
    shifted = values - centre
    variance = jnp.mean(shifted * shifted, axis=-1, keepdims=True)
    return shifted * lax.rsqrt(variance + norm_eps)


def dot(a, b):
    return lax.dot_general(a, b, (((1,), (0,)), ((), ())), preferred_element_type=F32)


def dot_last(a, b):
    return lax.dot_general(a, b, (((1,), (1,)), ((), ())), preferred_element_type=F32)


def dot_first(a, b):
    return lax.dot_general(a, b, (((0,), (0,)), ((), ())), preferred_element_type=F32)


def head_masks(rows, width, heads):
    lane = lax.broadcasted_iota(jnp.int32, (rows, width), 1)
    size = width // heads
    return [(lane >= h * size) & (lane < (h + 1) * size) for h in range(heads)]


def head_sums(values, masks):
    return [jnp.sum(jnp.where(m, values, 0.0), axis=1, keepdims=True) for m in masks]


def spread(columns, masks):
    total = jnp.zeros(masks[0].shape, F32)
    for column, m in zip(columns, masks):
        total = jnp.where(m, column, total)
    return total


def kernel(
    n_dp,
    n_seq,
    part,
    x_ref,
    taps_ref,
    ask_ref,
    look_ref,
    content_ref,
    read_ref,
    gain_ref,
    sens_ref,
    pooled_ref,
    update_ref,
    grads_ref,
    taps,
    x_wide,
    act,
    phases,
    kv,
    grads,
    grads_low,
    from_core,
    from_dp,
    from_z,
    low_dp,
    low_z,
    result,
    tap_send,
    tap_recv,
    tap_core_send,
    tap_core_recv,
    own_sem,
    halo_send,
    halo_recv,
    kv_send,
    kv_recv,
    kv_core_send,
    kv_core_recv,
    dp_send,
    dp_recv,
    z_send,
    z_recv,
    core_send,
    core_recv,
):
    d = lax.axis_index("dp")
    seq = lax.axis_index("seq")
    core = seq % 2
    z = seq // 2
    n_z = n_seq // 2
    partner = z * 2 + 1 - core
    nxt = (seq + 1) % n_seq
    prv = (seq + n_seq - 1) % n_seq
    other = core * nxt + (1 - core) * prv

    barrier = pltpu.get_barrier_semaphore()
    peers = [(d, partner), (d, other)]
    peers += [((d + k) % n_dp, seq) for k in range(1, n_dp)]
    peers += [(d, (z + k) % n_z * 2 + core) for k in range(1, n_z)]
    for peer in peers:
        pl.semaphore_signal(barrier, inc=1, device_id=peer, device_id_type=MESH)
    pl.semaphore_wait(barrier, len(peers))

    def remote(src, dst, send, recv, device):
        return pltpu.make_async_remote_copy(
            src_ref=src, dst_ref=dst, send_sem=send, recv_sem=recv,
            device_id=device, device_id_type=MESH,
        )

    n_taps, depth, width = taps_ref.shape
    half = width // 2
    side = math.isqrt(n_dp)
    a = (1 - core) * (d % side) + core * (d // side)
    b = (1 - core) * (d // side) + core * (d % side)

    def place(ai, bi, which):
        return (1 - which) * (bi * side + ai) + which * (ai * side + bi)

    def shard(owner, which):
        rows = pl.ds(pl.multiple_of(owner * depth, 16), depth)
        return taps.at[:, rows, pl.ds(pl.multiple_of(which * half, 128), half)]

    own_half = taps_ref.at[:, :, pl.ds(pl.multiple_of(core * half, 128), half)]
    tap_copies = []
    for k in range(1, side):
        c = remote(own_half, shard(d, core), tap_send.at[k, 0, 0], tap_recv.at[side - k, 0],
                   (place((a + k) % side, b, core), seq))
        c.start()
        tap_copies.append(c)
        c = remote(own_half, shard(d, core), tap_send.at[0, 0, k], tap_recv.at[0, side - k],
                   (place(a, (b + k) % side, core), seq))
        c.start()
        tap_copies.append(c)
    own_copy = pltpu.make_async_copy(
        taps_ref, taps.at[:, pl.ds(pl.multiple_of(d * depth, 16), depth), :], own_sem)
    own_copy.start()

    length = x_ref.shape[0]
    tokens = length // POOL
    groups = x_ref.shape[1] // LANES

    def activate_rows(i, carry):
        rows = pl.multiple_of(i * 64, 64)
        wide = x_ref[pl.ds(rows, 64), :].astype(F32)
        normal = layer_norm(wide)
        active = normal * jax.nn.sigmoid(1.702 * normal)
        for q in range(groups):
            x_wide[q, pl.ds(rows, 64), :] = wide[:, q * LANES : (q + 1) * LANES]
            act[q, pl.ds(rows + 8, 64), :] = active[:, q * LANES : (q + 1) * LANES]
        return carry

    lax.fori_loop(0, length // 64, activate_rows, 0)
    to_next = remote(act.at[:, pl.ds(length, 8)], act.at[:, pl.ds(0, 8)], halo_send.at[0],
                     halo_recv.at[0], (d, nxt))
    to_prev = remote(act.at[:, pl.ds(8, 8)], act.at[:, pl.ds(length + 8, 8)], halo_send.at[1],
                     halo_recv.at[1], (d, prv))
    to_next.start()
    to_prev.start()
    sens = sens_ref[...]
    readout = read_ref[...]
    heads_grad = dot_last(sens, readout).astype(BF16)
    to_next.wait()
    to_prev.wait()
    act[:, 0:8, :] = jnp.where(seq == 0, 0.0, act[:, 0:8, :])
    act[:, length + 8 : length + 16, :] = jnp.where(
        seq == n_seq - 1, 0.0, act[:, length + 8 : length + 16, :])
    margin = n_taps // 2
    for j in range(POOL + 2 * margin):
        for q in range(groups):
            phases[j * tokens : (j + 1) * tokens, q * LANES : (q + 1) * LANES] = act[
                q, pl.ds(8 - margin + j, tokens, stride=POOL), :].astype(BF16)

    core_copies = []

    def pass_on(i, j):
        owner = place((a + i) % side, (b + j) % side, core)
        piece = shard(owner, core)
        remote(piece, piece, tap_send.at[0, 0, 0], tap_recv.at[i, j], (d, partner)).wait_recv()
        if j == 0:
            for k in range(1, side):
                c = remote(piece, piece, tap_send.at[0, i, k], tap_recv.at[i, side - k],
                           (place(a, (b + k) % side, core), seq))
                c.start()
                tap_copies.append(c)
        c = remote(piece, piece, tap_core_send.at[i, j], tap_core_recv.at[i, j], (d, partner))
        c.start()
        core_copies.append(c)

    order = [(i, j) for j in range(side) for i in range(side) if (i, j) != (0, 0)]
    for i, j in order:
        pass_on(i, j)
    own_copy.wait()
    for c in core_copies:
        c.wait_recv()

    channels = phases.shape[1]
    step = 256
    for lo in range(0, width, step):
        total = dot(phases[0:length, :], taps[0, :, lo : lo + step])
        for t in range(1, n_taps):
            total = total + dot(
                phases[t * tokens : t * tokens + length, :], taps[t, :, lo : lo + step])
        best = None
        for j in range(POOL):
            parts = [x_wide[q, pl.ds(j, tokens, stride=POOL), :]
                     for q in range(lo // LANES, (lo + step) // LANES)]
            item = total[j * tokens : (j + 1) * tokens, :] + jnp.concatenate(parts, axis=1)
            best = item if best is None else jnp.maximum(best, item)
        pooled_ref[:, lo : lo + step] = best.astype(BF16)

    normed = layer_norm(pooled_ref[...].astype(F32)).astype(BF16)
    heads = gain_ref.shape[0]
    probe_width = ask_ref.shape[1]
    value_width = content_ref.shape[1]
    probe = probe_width // heads
    probe_masks = head_masks(tokens, probe_width, heads)
    value_masks = head_masks(tokens, value_width, heads)

    def head_factor(values):
        sums = head_sums(values * values, probe_masks)
        return spread([lax.rsqrt(s * (1.0 / probe) + head_eps) for s in sums], probe_masks)

    keys = dot(normed, look_ref[...])
    kv[seq, :, :probe_width] = (keys * head_factor(keys)).astype(BF16)
    kv[seq, :, probe_width:] = dot(normed, content_ref[...]).astype(BF16)

    def slot(chip, which):
        return kv.at[chip * 2 + which]

    def to_core(chip, index):
        piece = slot(chip, core)
        return remote(piece, piece, kv_core_send.at[index], kv_core_recv.at[index], (d, partner))

    def up(s):
        piece = slot(jnp.maximum(z - s, 0), core)
        return remote(piece, piece, kv_send.at[0, s], kv_recv.at[0, s],
                      (d, (z + 1) % n_z * 2 + core))

    def down(s):
        piece = slot(jnp.minimum(z + s, n_z - 1), core)
        return remote(piece, piece, kv_send.at[1, s], kv_recv.at[1, s],
                      (d, (z + n_z - 1) % n_z * 2 + core))

    @pl.when(z + 1 < n_z)
    def _():
        up(0).start()

    @pl.when(z >= 1)
    def _():
        down(0).start()

    to_core(z, 0).start()

    queries = dot(normed, ask_ref[...])
    query_factor = head_factor(queries)
    query_hat = queries * query_factor
    query_unit = query_hat.astype(BF16)

    for s in range(1, n_z):
        @pl.when(z - s >= 0)
        def _():
            up(s - 1).wait_recv()

            @pl.when(z + 1 < n_z)
            def _():
                up(s).start()

            to_core(jnp.maximum(z - s, 0), s).start()

        @pl.when(z + s < n_z)
        def _():
            down(s - 1).wait_recv()

            @pl.when(z >= 1)
            def _():
                down(s).start()

            to_core(jnp.minimum(z + s, n_z - 1), n_z - 1 + s).start()

    to_core(z, 0).wait()
    for s in range(1, n_z):
        @pl.when(z - s >= 0)
        def _():
            to_core(jnp.maximum(z - s, 0), s).wait()

            @pl.when(z + 1 < n_z)
            def _():
                up(s).wait_send()

        @pl.when(z + s < n_z)
        def _():
            to_core(jnp.minimum(z + s, n_z - 1), n_z - 1 + s).wait()

            @pl.when(z >= 1)
            def _():
                down(s).wait_send()

    @pl.when(z + 1 < n_z)
    def _():
        up(0).wait_send()

    @pl.when(z >= 1)
    def _():
        down(0).wait_send()

    every = n_seq * tokens
    key_all = kv[:, :, :probe_width].reshape(every, probe_width)
    value_all = kv[:, :, probe_width:].reshape(every, value_width)
    heads_out = jnp.zeros((tokens, value_width), F32)
    unit_grad = jnp.zeros((tokens, probe_width), F32)
    zero = jnp.zeros((), BF16)
    for h in range(heads):
        gain = gain_ref[h] * (1.0 / probe)
        scores = dot_last(jnp.where(probe_masks[h], query_unit, zero), key_all) * gain
        expo = jnp.exp(scores)
        probs = expo * (1.0 / jnp.sum(expo, axis=1, keepdims=True))
        head_out = dot(probs.astype(BF16), value_all)
        heads_out = jnp.where(value_masks[h], head_out, heads_out)
        grad_part = jnp.where(value_masks[h], heads_grad, zero)
        prob_grad = dot_last(grad_part, value_all)
        delta = jnp.sum(grad_part.astype(F32) * head_out, axis=1, keepdims=True)
        score_grad = (probs * (prob_grad - delta)).astype(BF16)
        unit_grad = jnp.where(probe_masks[h], dot(score_grad, key_all) * gain, unit_grad)
    heads_low = heads_out.astype(BF16)
    means = [s * (1.0 / probe) for s in head_sums(query_hat * unit_grad, probe_masks)]
    query_diff = (query_factor * (unit_grad - query_hat * spread(means, probe_masks))).astype(BF16)

    block = probe_width
    grads[0:channels, :] = dot_first(normed, query_diff)
    out_local = dot_first(heads_low, sens)
    base = channels
    for lo in range(0, width, block):
        grads[base : base + value_width, :] = out_local[:, lo : lo + block]
        base += value_width
    if base < grads.shape[0]:
        grads[base:, :] = jnp.zeros((grads.shape[0] - base, block), F32)
    core_rows = n_dp * n_z * part
    dp_rows = n_z * part

    def rows_of(start, count):
        return pl.ds(pl.multiple_of(start, 16), count)

    mine = rows_of(core * core_rows, core_rows)
    theirs = rows_of((1 - core) * core_rows, core_rows)
    grads_low[...] = grads[theirs, :].astype(BF16)
    swap = remote(grads_low, from_core, core_send.at[0], core_recv.at[0], (d, partner))
    swap.start()
    update_ref[...] = dot(heads_low, readout)
    swap.wait()
    sums = grads[mine, :] + from_core[...].astype(F32)
    grads[0:core_rows, :] = sums
    low_dp[...] = sums.astype(BF16)
    copies = []
    for k in range(1, n_dp):
        peer = (d + k) % n_dp
        c = remote(low_dp.at[rows_of(peer * dp_rows, dp_rows)], from_dp.at[n_dp - k],
                   dp_send.at[0, k], dp_recv.at[0, n_dp - k], (peer, seq))
        c.start()
        copies.append(c)
    for c in copies:
        c.wait()
    sums = grads[rows_of(d * dp_rows, dp_rows), :]
    for k in range(1, n_dp):
        sums = sums + from_dp[k].astype(F32)
    grads[0:dp_rows, :] = sums
    low_z[...] = sums.astype(BF16)
    copies = []
    for k in range(1, n_z):
        peer = (z + k) % n_z
        c = remote(low_z.at[rows_of(peer * part, part)], from_z.at[n_z - k],
                   z_send.at[0, k], z_recv.at[0, n_z - k], (d, peer * 2 + core))
        c.start()
        copies.append(c)
    for c in copies:
        c.wait()
    sums = grads[rows_of(z * part, part), :]
    for k in range(1, n_z):
        sums = sums + from_z[k].astype(F32)
    first = core * core_rows + d * dp_rows
    own = rows_of(first + z * part, part)
    result[own, :] = sums.astype(BF16)
    copies = []
    for k in range(1, n_z):
        c = remote(result.at[own], result.at[own], z_send.at[1, k], z_recv.at[1, n_z - k],
                   (d, (z + k) % n_z * 2 + core))
        c.start()
        copies.append(c)
    for c in copies:
        c.wait()
    own = rows_of(first, dp_rows)
    copies = []
    for k in range(1, n_dp):
        c = remote(result.at[own], result.at[own], dp_send.at[1, k], dp_recv.at[1, n_dp - k],
                   ((d + k) % n_dp, seq))
        c.start()
        copies.append(c)
    for c in copies:
        c.wait()
    swap = remote(result.at[mine], result.at[mine], core_send.at[1], core_recv.at[1], (d, partner))
    swap.start()
    for c in tap_copies:
        c.wait_send()
    for c in core_copies:
        c.wait_send()
    swap.wait()
    grads_ref[...] = result[...]


def on_device(n_dp, n_seq, x, taps, ask, look, content, read, gain, sens):
    x = x[0]
    sens = sens[0]
    length, channels = x.shape
    n_taps, depth, width = taps.shape
    tokens = length // POOL
    probe_width = ask.shape[1]
    value_width = content.shape[1]
    n_z = n_seq // 2
    side = math.isqrt(n_dp)
    devices = n_dp * n_seq
    real_rows = channels + value_width * (width // probe_width)
    part = -(-real_rows // (devices * 16)) * 16
    total_rows = part * devices
    core_rows = total_rows // 2
    dp_rows = core_rows // n_dp
    vmem = pl.BlockSpec(memory_space=pltpu.VMEM)
    dma = pltpu.SemaphoreType.DMA
    pooled, update, grads = pl.pallas_call(
        functools.partial(kernel, n_dp, n_seq, part),
        out_shape=(
            jax.ShapeDtypeStruct((tokens, width), BF16),
            jax.ShapeDtypeStruct((tokens, width), F32),
            jax.ShapeDtypeStruct((total_rows, probe_width), BF16),
        ),
        in_specs=[
            vmem, pl.BlockSpec(memory_space=pl.ANY), vmem, vmem, vmem, vmem,
            pl.BlockSpec(memory_space=pltpu.SMEM), vmem,
        ],
        out_specs=(vmem, vmem, vmem),
        scratch_shapes=[
            pltpu.VMEM((n_taps, channels, width), BF16),
            pltpu.VMEM((channels // LANES, length, LANES), F32),
            pltpu.VMEM((channels // LANES, length + 16, LANES), F32),
            pltpu.VMEM(((POOL + 2 * (n_taps // 2)) * tokens, channels), BF16),
            pltpu.VMEM((n_seq, tokens, probe_width + value_width), BF16),
            pltpu.VMEM((total_rows, probe_width), F32),
            pltpu.VMEM((core_rows, probe_width), BF16),
            pltpu.VMEM((core_rows, probe_width), BF16),
            pltpu.VMEM((n_dp, dp_rows, probe_width), BF16),
            pltpu.VMEM((n_z, part, probe_width), BF16),
            pltpu.VMEM((core_rows, probe_width), BF16),
            pltpu.VMEM((dp_rows, probe_width), BF16),
            pltpu.VMEM((total_rows, probe_width), BF16),
            dma((side, side, side)),
            dma((side, side)),
            dma((side, side)),
            dma((side, side)),
            dma,
            dma((2,)),
            dma((2,)),
            dma((2, n_z)),
            dma((2, n_z)),
            dma((2 * n_z,)),
            dma((2 * n_z,)),
            dma((2, n_dp)),
            dma((2, n_dp)),
            dma((2, n_z)),
            dma((2, n_z)),
            dma((2,)),
            dma((2,)),
        ],
        compiler_params=pltpu.CompilerParams(
            collective_id=0, has_side_effects=True, vmem_limit_bytes=58 * 1024 * 1024
        ),
    )(x, taps, ask, look, content, read, gain, sens)
    query_grad = grads[:channels].astype(F32)
    blocks = grads[channels:real_rows].reshape(width // probe_width, value_width, probe_width)
    out_grad = jnp.concatenate(list(blocks), axis=1).astype(F32)
    return pooled[None], update[None], query_grad, out_grad


def solution(mesh):
    return jax.shard_map(
        functools.partial(on_device, mesh.shape["dp"], mesh.shape["seq"]),
        mesh=mesh,
        in_specs=(
            P("dp", "seq", None),
            P(None, "dp", None),
            P(),
            P(),
            P(),
            P(),
            P(),
            P("dp", "seq", None),
        ),
        out_specs=(P("dp", "seq", None), P("dp", "seq", None), P(), P()),
        check_vma=False,
    )
```

```python
import functools
import math

import jax
import jax.numpy as jnp
from jax import lax
from jax.experimental import pallas as pl
from jax.experimental.pallas import tpu as pltpu
from jax.sharding import PartitionSpec as P

POOL = 4
LANES = 128
norm_eps = 1e-05
head_eps = 1e-06
F32 = jnp.float32
BF16 = jnp.bfloat16
MESH = pl.DeviceIdType.MESH


def layer_norm(values):
    centre = jnp.mean(values, axis=-1, keepdims=True)
    shifted = values - centre
    variance = jnp.mean(shifted * shifted, axis=-1, keepdims=True)
    return shifted * lax.rsqrt(variance + norm_eps)


def dot(a, b):
    return lax.dot_general(a, b, (((1,), (0,)), ((), ())), preferred_element_type=F32)


def dot_last(a, b):
    return lax.dot_general(a, b, (((1,), (1,)), ((), ())), preferred_element_type=F32)


def dot_first(a, b):
    return lax.dot_general(a, b, (((0,), (0,)), ((), ())), preferred_element_type=F32)


def head_masks(rows, width, heads):
    lane = lax.broadcasted_iota(jnp.int32, (rows, width), 1)
    size = width // heads
    return [(lane >= h * size) & (lane < (h + 1) * size) for h in range(heads)]


def head_sums(values, masks):
    return [jnp.sum(jnp.where(m, values, 0.0), axis=1, keepdims=True) for m in masks]


def spread(columns, masks):
    total = jnp.zeros(masks[0].shape, F32)
    for column, m in zip(columns, masks):
        total = jnp.where(m, column, total)
    return total


def kernel(
    n_dp,
    n_seq,
    part,
    x_ref,
    taps_ref,
    ask_ref,
    look_ref,
    content_ref,
    read_ref,
    gain_ref,
    sens_ref,
    pooled_ref,
    update_ref,
    grads_ref,
    taps,
    x_wide,
    act,
    phases,
    kv,
    grads,
    grads_low,
    from_core,
    from_dp,
    from_z,
    low_dp,
    low_z,
    result,
    tap_send,
    tap_recv,
    tap_core_send,
    tap_core_recv,
    tap_z_send,
    tap_z_recv,
    own_sem,
    halo_send,
    halo_recv,
    kv_send,
    kv_recv,
    kv_core_send,
    kv_core_recv,
    dp_send,
    dp_recv,
    z_send,
    z_recv,
    core_send,
    core_recv,
):
    d = lax.axis_index("dp")
    seq = lax.axis_index("seq")
    core = seq % 2
    z = seq // 2
    n_z = n_seq // 2
    partner = z * 2 + 1 - core
    nxt = (seq + 1) % n_seq
    prv = (seq + n_seq - 1) % n_seq
    other = core * nxt + (1 - core) * prv

    n_taps, depth, width = taps_ref.shape
    n_blocks = taps.shape[1]
    cols = width // n_blocks

    def rows_of(start, count):
        return pl.ds(pl.multiple_of(start, 16), count)

    own_copies = [
        pltpu.make_async_copy(
            taps_ref.at[:, :, m * cols : (m + 1) * cols],
            taps.at[:, m, rows_of(d * depth, depth), :], own_sem.at[m])
        for m in range(n_blocks)
    ]
    for c in own_copies:
        c.start()

    barrier = pltpu.get_barrier_semaphore()
    peers = [(d, partner), (d, other)]
    peers += [((d + k) % n_dp, seq) for k in range(1, n_dp)]
    peers += [(d, (z + k) % n_z * 2 + core) for k in range(1, n_z)]
    for peer in peers:
        pl.semaphore_signal(barrier, inc=1, device_id=peer, device_id_type=MESH)
    pl.semaphore_wait(barrier, len(peers))

    def remote(src, dst, send, recv, device):
        return pltpu.make_async_remote_copy(
            src_ref=src, dst_ref=dst, send_sem=send, recv_sem=recv,
            device_id=device, device_id_type=MESH,
        )

    side = math.isqrt(n_dp)
    a = (1 - core) * (d % side) + core * (d // side)
    b = (1 - core) * (d // side) + core * (d % side)

    def place(ai, bi, which):
        return (1 - which) * (bi * side + ai) + which * (ai * side + bi)

    parity = z % 2
    pair = z + 1 - 2 * parity
    thirds = [1 + parity, 0, 2 - parity]

    def piece(owner, u):
        return taps.at[:, thirds[u] * 2 + core, rows_of(owner * depth, depth), :]

    tap_copies = []
    core_copies = {}

    def direct(u):
        own = piece(d, u)
        for k in range(1, side):
            tap_copies.append(remote(
                own, own, tap_send.at[u, 0, 0, k], tap_recv.at[u, side - k, 0],
                (place((a + k) % side, b, core), seq)))
            tap_copies[-1].start()
            tap_copies.append(remote(
                own, own, tap_send.at[u, 1, 0, k], tap_recv.at[u, 0, side - k],
                (place(a, (b + k) % side, core), seq)))
            tap_copies[-1].start()

    def owner_of(i, j):
        return place((a + i) % side, (b + j) % side, core)

    def cross(u, i, j):
        own = piece(owner_of(i, j), u)
        core_copies[u, i, j] = remote(
            own, own, tap_core_send.at[u, i, j], tap_core_recv.at[u, i, j], (d, partner))
        core_copies[u, i, j].start()

    z_copies = {}

    def pass_on(u, i, j):
        own = piece(owner_of(i, j), u)
        remote(own, own, tap_send.at[u, 0, 0, 0], tap_recv.at[u, i, j], (d, partner)).wait_recv()
        if j == 0:
            for k in range(1, side):
                tap_copies.append(remote(
                    own, own, tap_send.at[u, 1, i, k], tap_recv.at[u, i, side - k],
                    (place(a, (b + k) % side, core), seq)))
                tap_copies[-1].start()
        if u == 0:
            z_copies[i, j] = remote(
                own, own, tap_z_send.at[i, j], tap_z_recv.at[i, j], (d, pair * 2 + core))
            z_copies[i, j].start()
        cross(u, i, j)

    for c in own_copies:
        c.wait()
    direct(0)

    length = x_ref.shape[0]
    tokens = length // POOL
    groups = x_ref.shape[1] // LANES

    def activate_rows(i, carry):
        rows = pl.multiple_of(i * 64, 64)
        wide = x_ref[pl.ds(rows, 64), :].astype(F32)
        normal = layer_norm(wide)
        active = normal * jax.nn.sigmoid(1.702 * normal)
        for q in range(groups):
            x_wide[q, pl.ds(rows, 64), :] = wide[:, q * LANES : (q + 1) * LANES]
            act[q, pl.ds(rows + 8, 64), :] = active[:, q * LANES : (q + 1) * LANES]
        return carry

    lax.fori_loop(0, length // 64, activate_rows, 0)
    to_next = remote(act.at[:, pl.ds(length, 8)], act.at[:, pl.ds(0, 8)], halo_send.at[0],
                     halo_recv.at[0], (d, nxt))
    to_prev = remote(act.at[:, pl.ds(8, 8)], act.at[:, pl.ds(length + 8, 8)], halo_send.at[1],
                     halo_recv.at[1], (d, prv))
    to_next.start()
    to_prev.start()
    sens = sens_ref[...]
    readout = read_ref[...]
    heads_grad = dot_last(sens, readout).astype(BF16)
    to_next.wait()
    to_prev.wait()
    act[:, 0:8, :] = jnp.where(seq == 0, 0.0, act[:, 0:8, :])
    act[:, length + 8 : length + 16, :] = jnp.where(
        seq == n_seq - 1, 0.0, act[:, length + 8 : length + 16, :])
    margin = n_taps // 2
    for j in range(POOL + 2 * margin):
        for q in range(groups):
            phases[j * tokens : (j + 1) * tokens, q * LANES : (q + 1) * LANES] = act[
                q, pl.ds(8 - margin + j, tokens, stride=POOL), :].astype(BF16)

    first = [(i, 0) for i in range(1, side)]
    second = [(0, j) for j in range(1, side)]
    third = [(i, j) for j in range(1, side) for i in range(1, side)]
    channels = phases.shape[1]

    def convolve(u):
        for at in first + second + third:
            core_copies[(u,) + at].wait_recv()
        step = 2 * cols
        lo = thirds[u] * 2
        total = None
        for t in range(n_taps):
            weight = jnp.concatenate([taps[t, lo], taps[t, lo + 1]], axis=1)
            term = dot(phases[t * tokens : t * tokens + length, :], weight)
            total = term if total is None else total + term
        best = None
        for j in range(POOL):
            rows = pl.ds(j, tokens, stride=POOL)
            parts = [x_wide[thirds[u] * (step // LANES) + q, rows, :] for q in range(step // LANES)]
            item = total[j * tokens : (j + 1) * tokens, :] + jnp.concatenate(parts, axis=1)
            best = item if best is None else jnp.maximum(best, item)
        pooled_ref[:, pl.ds(pl.multiple_of(thirds[u] * step, 128), step)] = best.astype(BF16)

    for i, j in first + second:
        pass_on(0, i, j)
    direct(1)
    for i, j in third:
        pass_on(0, i, j)
    for i, j in first + second:
        pass_on(1, i, j)
    convolve(0)

    def from_pair(i, j):
        z_copies[i, j].wait_recv()
        cross(2, i, j)

    for i, j in third:
        pass_on(1, i, j)
    for i, j in first + second:
        from_pair(i, j)
    convolve(1)
    for i, j in third:
        from_pair(i, j)
    convolve(2)

    normed = layer_norm(pooled_ref[...].astype(F32)).astype(BF16)
    heads = gain_ref.shape[0]
    probe_width = ask_ref.shape[1]
    value_width = content_ref.shape[1]
    probe = probe_width // heads
    probe_masks = head_masks(tokens, probe_width, heads)
    value_masks = head_masks(tokens, value_width, heads)

    def head_factor(values):
        sums = head_sums(values * values, probe_masks)
        return spread([lax.rsqrt(s * (1.0 / probe) + head_eps) for s in sums], probe_masks)

    keys = dot(normed, look_ref[...])
    kv[seq, :, :probe_width] = (keys * head_factor(keys)).astype(BF16)
    kv[seq, :, probe_width:] = dot(normed, content_ref[...]).astype(BF16)

    def slot(chip, which):
        return kv.at[chip * 2 + which]

    def to_core(chip, index):
        piece = slot(chip, core)
        return remote(piece, piece, kv_core_send.at[index], kv_core_recv.at[index], (d, partner))

    def up(s):
        piece = slot(jnp.maximum(z - s, 0), core)
        return remote(piece, piece, kv_send.at[0, s], kv_recv.at[0, s],
                      (d, (z + 1) % n_z * 2 + core))

    def down(s):
        piece = slot(jnp.minimum(z + s, n_z - 1), core)
        return remote(piece, piece, kv_send.at[1, s], kv_recv.at[1, s],
                      (d, (z + n_z - 1) % n_z * 2 + core))

    @pl.when(z + 1 < n_z)
    def _():
        up(0).start()

    @pl.when(z >= 1)
    def _():
        down(0).start()

    to_core(z, 0).start()

    queries = dot(normed, ask_ref[...])
    query_factor = head_factor(queries)
    query_hat = queries * query_factor
    query_unit = query_hat.astype(BF16)

    for s in range(1, n_z):
        @pl.when(z - s >= 0)
        def _():
            up(s - 1).wait_recv()

            @pl.when(z + 1 < n_z)
            def _():
                up(s).start()

            to_core(jnp.maximum(z - s, 0), s).start()

        @pl.when(z + s < n_z)
        def _():
            down(s - 1).wait_recv()

            @pl.when(z >= 1)
            def _():
                down(s).start()

            to_core(jnp.minimum(z + s, n_z - 1), n_z - 1 + s).start()

    to_core(z, 0).wait()
    for s in range(1, n_z):
        @pl.when(z - s >= 0)
        def _():
            to_core(jnp.maximum(z - s, 0), s).wait()

            @pl.when(z + 1 < n_z)
            def _():
                up(s).wait_send()

        @pl.when(z + s < n_z)
        def _():
            to_core(jnp.minimum(z + s, n_z - 1), n_z - 1 + s).wait()

            @pl.when(z >= 1)
            def _():
                down(s).wait_send()

    @pl.when(z + 1 < n_z)
    def _():
        up(0).wait_send()

    @pl.when(z >= 1)
    def _():
        down(0).wait_send()

    every = n_seq * tokens
    key_all = kv[:, :, :probe_width].reshape(every, probe_width)
    value_all = kv[:, :, probe_width:].reshape(every, value_width)
    heads_out = jnp.zeros((tokens, value_width), F32)
    unit_grad = jnp.zeros((tokens, probe_width), F32)
    zero = jnp.zeros((), BF16)
    for h in range(heads):
        gain = gain_ref[h] * (1.0 / probe)
        scores = dot_last(jnp.where(probe_masks[h], query_unit, zero), key_all) * gain
        expo = jnp.exp(scores)
        probs = expo * (1.0 / jnp.sum(expo, axis=1, keepdims=True))
        head_out = dot(probs.astype(BF16), value_all)
        heads_out = jnp.where(value_masks[h], head_out, heads_out)
        grad_part = jnp.where(value_masks[h], heads_grad, zero)
        prob_grad = dot_last(grad_part, value_all)
        delta = jnp.sum(grad_part.astype(F32) * head_out, axis=1, keepdims=True)
        score_grad = (probs * (prob_grad - delta)).astype(BF16)
        unit_grad = jnp.where(probe_masks[h], dot(score_grad, key_all) * gain, unit_grad)
    heads_low = heads_out.astype(BF16)
    means = [s * (1.0 / probe) for s in head_sums(query_hat * unit_grad, probe_masks)]
    query_diff = (query_factor * (unit_grad - query_hat * spread(means, probe_masks))).astype(BF16)

    block = probe_width
    grads[0:channels, :] = dot_first(normed, query_diff)
    out_local = dot_first(heads_low, sens)
    base = channels
    for lo in range(0, width, block):
        grads[base : base + value_width, :] = out_local[:, lo : lo + block]
        base += value_width
    if base < grads.shape[0]:
        grads[base:, :] = jnp.zeros((grads.shape[0] - base, block), F32)
    core_rows = n_dp * n_z * part
    dp_rows = n_z * part

    mine = rows_of(core * core_rows, core_rows)
    theirs = rows_of((1 - core) * core_rows, core_rows)
    grads_low[...] = grads[theirs, :].astype(BF16)
    swap = remote(grads_low, from_core, core_send.at[0], core_recv.at[0], (d, partner))
    swap.start()
    update_ref[...] = dot(heads_low, readout)
    swap.wait()
    sums = grads[mine, :] + from_core[...].astype(F32)
    grads[0:core_rows, :] = sums
    low_dp[...] = sums.astype(BF16)
    copies = []
    for k in range(1, n_dp):
        peer = (d + k) % n_dp
        c = remote(low_dp.at[rows_of(peer * dp_rows, dp_rows)], from_dp.at[n_dp - k],
                   dp_send.at[0, k], dp_recv.at[0, n_dp - k], (peer, seq))
        c.start()
        copies.append(c)
    for c in copies:
        c.wait()
    sums = grads[rows_of(d * dp_rows, dp_rows), :]
    for k in range(1, n_dp):
        sums = sums + from_dp[k].astype(F32)
    grads[0:dp_rows, :] = sums
    low_z[...] = sums.astype(BF16)
    copies = []
    for k in range(1, n_z):
        peer = (z + k) % n_z
        c = remote(low_z.at[rows_of(peer * part, part)], from_z.at[n_z - k],
                   z_send.at[0, k], z_recv.at[0, n_z - k], (d, peer * 2 + core))
        c.start()
        copies.append(c)
    for c in copies:
        c.wait()
    sums = grads[rows_of(z * part, part), :]
    for k in range(1, n_z):
        sums = sums + from_z[k].astype(F32)
    first = core * core_rows + d * dp_rows
    own = rows_of(first + z * part, part)
    result[own, :] = sums.astype(BF16)
    copies = []
    for k in range(1, n_z):
        c = remote(result.at[own], result.at[own], z_send.at[1, k], z_recv.at[1, n_z - k],
                   (d, (z + k) % n_z * 2 + core))
        c.start()
        copies.append(c)
    for c in copies:
        c.wait()
    own = rows_of(first, dp_rows)
    copies = []
    for k in range(1, n_dp):
        c = remote(result.at[own], result.at[own], dp_send.at[1, k], dp_recv.at[1, n_dp - k],
                   ((d + k) % n_dp, seq))
        c.start()
        copies.append(c)
    for c in copies:
        c.wait()
    swap = remote(result.at[mine], result.at[mine], core_send.at[1], core_recv.at[1], (d, partner))
    swap.start()
    for c in tap_copies:
        c.wait_send()
    for c in list(core_copies.values()) + list(z_copies.values()):
        c.wait_send()
    swap.wait()
    grads_ref[...] = result[...]


def finish(pooled_in, update_in, grads_in, pooled_ref, update_ref, query_ref, out_ref):
    pooled_ref[...] = pooled_in[...]
    update_ref[...] = update_in[...]
    base = query_ref.shape[0]
    query_ref[...] = grads_in[0:base, :].astype(F32)
    rows, width = out_ref.shape
    block = query_ref.shape[1]
    for lo in range(0, width, block):
        out_ref[:, lo : lo + block] = grads_in[base : base + rows, :].astype(F32)
        base += rows


def on_device(n_dp, n_seq, x, taps, ask, look, content, read, gain, sens):
    x = x[0]
    sens = sens[0]
    length, channels = x.shape
    n_taps, depth, width = taps.shape
    tokens = length // POOL
    probe_width = ask.shape[1]
    value_width = content.shape[1]
    n_z = n_seq // 2
    side = math.isqrt(n_dp)
    devices = n_dp * n_seq
    real_rows = channels + value_width * (width // probe_width)
    part = -(-real_rows // (devices * 16)) * 16
    total_rows = part * devices
    core_rows = total_rows // 2
    dp_rows = core_rows // n_dp
    blocks = 6
    vmem = pl.BlockSpec(memory_space=pltpu.VMEM)
    dma = pltpu.SemaphoreType.DMA
    pooled, update, grads = pl.pallas_call(
        functools.partial(kernel, n_dp, n_seq, part),
        out_shape=(
            jax.ShapeDtypeStruct((tokens, width), BF16),
            jax.ShapeDtypeStruct((tokens, width), F32),
            jax.ShapeDtypeStruct((total_rows, probe_width), BF16),
        ),
        in_specs=[
            vmem, pl.BlockSpec(memory_space=pl.ANY), vmem, vmem, vmem, vmem,
            pl.BlockSpec(memory_space=pltpu.SMEM), vmem,
        ],
        out_specs=(vmem, vmem, vmem),
        scratch_shapes=[
            pltpu.VMEM((n_taps, blocks, channels, width // blocks), BF16),
            pltpu.VMEM((channels // LANES, length, LANES), F32),
            pltpu.VMEM((channels // LANES, length + 16, LANES), F32),
            pltpu.VMEM(((POOL + 2 * (n_taps // 2)) * tokens, channels), BF16),
            pltpu.VMEM((n_seq, tokens, probe_width + value_width), BF16),
            pltpu.VMEM((total_rows, probe_width), F32),
            pltpu.VMEM((core_rows, probe_width), BF16),
            pltpu.VMEM((core_rows, probe_width), BF16),
            pltpu.VMEM((n_dp, dp_rows, probe_width), BF16),
            pltpu.VMEM((n_z, part, probe_width), BF16),
            pltpu.VMEM((core_rows, probe_width), BF16),
            pltpu.VMEM((dp_rows, probe_width), BF16),
            pltpu.VMEM((total_rows, probe_width), BF16),
            dma((2, 2, side, side)),
            dma((2, side, side)),
            dma((3, side, side)),
            dma((3, side, side)),
            dma((side, side)),
            dma((side, side)),
            dma((blocks,)),
            dma((2,)),
            dma((2,)),
            dma((2, n_z)),
            dma((2, n_z)),
            dma((2 * n_z,)),
            dma((2 * n_z,)),
            dma((2, n_dp)),
            dma((2, n_dp)),
            dma((2, n_z)),
            dma((2, n_z)),
            dma((2,)),
            dma((2,)),
        ],
        compiler_params=pltpu.CompilerParams(
            collective_id=0, has_side_effects=True, vmem_limit_bytes=58 * 1024 * 1024
        ),
    )(x, taps, ask, look, content, read, gain, sens)
    pooled, update, query_grad, out_grad = pl.pallas_call(
        finish,
        out_shape=(
            jax.ShapeDtypeStruct((tokens, width), BF16),
            jax.ShapeDtypeStruct((tokens, width), F32),
            jax.ShapeDtypeStruct((channels, probe_width), F32),
            jax.ShapeDtypeStruct((value_width, width), F32),
        ),
        in_specs=[vmem, vmem, vmem],
        out_specs=(vmem, vmem, vmem, vmem),
        compiler_params=pltpu.CompilerParams(vmem_limit_bytes=40 * 1024 * 1024),
    )(pooled, update, grads)
    return pooled[None], update[None], query_grad, out_grad


def solution(mesh):
    return jax.shard_map(
        functools.partial(on_device, mesh.shape["dp"], mesh.shape["seq"]),
        mesh=mesh,
        in_specs=(
            P("dp", "seq", None),
            P(None, "dp", None),
            P(),
            P(),
            P(),
            P(),
            P(),
            P("dp", "seq", None),
        ),
        out_specs=(P("dp", "seq", None), P("dp", "seq", None), P(), P()),
        check_vma=False,
    )
```
